32 devices in a mesh: batch: 2 (over core), ctx: 16 (over z, y, x).
Axes of the slice: x: 2, y: 2, z: 4, core: 2. Of those that a mesh axis runs over, the one named last changes fastest.
Arguments:
- inputs: bfloat16 [2, 2, 1536, 1024], P(None, 'batch', 'ctx'), may hold values from -6 to 6
- cotangent: bfloat16 [2, 2, 1536, 1024], P(None, 'batch', 'ctx'), may hold values from -6 to 6
- routes: int32 [2, 2, 1536, 8], P(None, 'batch'), may hold values from 0 to 15, all different within a row
- segments: int32 [2, 2, 1536], P(None, 'batch'), may hold values from 0 to 5, as said below
- gains: float32 [2, 1024], P(None, ('batch', 'ctx')), may hold values from 0.5 to 1.5
- gains_first: float32 [2, 1024], P(None, ('batch', 'ctx')), may hold values from -80 to 80
- gains_second: float32 [2, 1024], P(None, ('batch', 'ctx')), may hold values from 356.352 to 5836.8
- w_query: float32 [1024, 1024], P(('batch', 'ctx')), may hold values from -0.1875 to 0.1875
- query_first: float32 [1024, 1024], P(('batch', 'ctx')), may hold values from -80 to 80
- query_second: float32 [1024, 1024], P(('batch', 'ctx')), may hold values from 356.352 to 5836.8
- w_keyvalue: float32 [1024, 1024], P(('batch', 'ctx')), may hold values from -0.1875 to 0.1875
- keyvalue_first: float32 [1024, 1024], P(('batch', 'ctx')), may hold values from -80 to 80
- keyvalue_second: float32 [1024, 1024], P(('batch', 'ctx')), may hold values from 356.352 to 5836.8
- w_out: float32 [1024, 1024], P(('batch', 'ctx')), may hold values from -1.5 to 1.5
- out_first: float32 [1024, 1024], P(('batch', 'ctx')), may hold values from -5 to 5
- out_second: float32 [1024, 1024], P(('batch', 'ctx')), may hold values from 1.59744 to 25.8048
- w_router: float32 [1024, 16], P(('batch', 'ctx')), may hold values from -0.09375 to 0.09375
- router_first: float32 [1024, 16], P(('batch', 'ctx')), may hold values from -384 to 384
- router_second: float32 [1024, 16], P(('batch', 'ctx')), may hold values from 7802.88 to 126566.4
- w_gate_up: float32 [16, 1024, 1024], P(None, ('batch', 'ctx')), may hold values from -0.1875 to 0.1875
- gate_up_first: float32 [16, 1024, 1024], P(None, ('batch', 'ctx')), may hold values from -16 to 16
- gate_up_second: float32 [16, 1024, 1024], P(None, ('batch', 'ctx')), may hold values from 19.6608 to 313.344
- w_down: float32 [16, 1024, 512], P(None, ('batch', 'ctx')), may hold values from -1 to 1
- down_first: float32 [16, 1024, 512], P(None, ('batch', 'ctx')), may hold values from -3 to 3
- down_second: float32 [16, 1024, 512], P(None, ('batch', 'ctx')), may hold values from 0.577536 to 9.216
Outputs:
- outputs: bfloat16 [2, 2, 1536, 1024], P(None, 'batch', 'ctx')
- input_grad: float32 [2, 2, 1536, 1024], P(None, 'batch', 'ctx')
- gains_moment: float32 [2, 1024], P(None, ('batch', 'ctx'))
- gains_square: float32 [2, 1024], P(None, ('batch', 'ctx'))
- gains_new: float32 [2, 1024], P(None, ('batch', 'ctx'))
- query_moment: float32 [1024, 1024], P(('batch', 'ctx'))
- query_square: float32 [1024, 1024], P(('batch', 'ctx'))
- query_new: float32 [1024, 1024], P(('batch', 'ctx'))
- keyvalue_moment: float32 [1024, 1024], P(('batch', 'ctx'))
- keyvalue_square: float32 [1024, 1024], P(('batch', 'ctx'))
- keyvalue_new: float32 [1024, 1024], P(('batch', 'ctx'))
- out_moment: float32 [1024, 1024], P(('batch', 'ctx'))
- out_square: float32 [1024, 1024], P(('batch', 'ctx'))
- out_new: float32 [1024, 1024], P(('batch', 'ctx'))
- router_moment: float32 [1024, 16], P(('batch', 'ctx'))
- router_square: float32 [1024, 16], P(('batch', 'ctx'))
- router_new: float32 [1024, 16], P(('batch', 'ctx'))
- gate_up_moment: float32 [16, 1024, 1024], P(None, ('batch', 'ctx'))
- gate_up_square: float32 [16, 1024, 1024], P(None, ('batch', 'ctx'))
- gate_up_new: float32 [16, 1024, 1024], P(None, ('batch', 'ctx'))
- down_moment: float32 [16, 1024, 512], P(None, ('batch', 'ctx'))
- down_square: float32 [16, 1024, 512], P(None, ('batch', 'ctx'))
- down_new: float32 [16, 1024, 512], P(None, ('batch', 'ctx'))
The draws below stay inside these ranges and needn't reach their ends.
Inputs may be any that keep to these rules, and one draw needn't show every extreme that they name: `routes`: each token names 8 different experts. `segments`: within a sequence the numbers never fall and start at 0. For each index of the second dimension, one of the 2 micro-batches (first dimension), drawn from the seed, holds a single-document sequence; the other holds 6 documents.
All inputs are finite; a program needn't handle non-finite values.
Results may differ from the reference program's by a relative error of at most 0.03.
Values may be sent and summed in bfloat16 or wider, within the bound.
A program may use at most 384 MiB of HBM per device.

```python
import math
import jax
import jax.numpy as jnp
from jax import lax

D = 1024
HEADS = 16
KV_HEADS = 8
HEAD_DIM = 64
FF = 512
EXPERTS = 16
TOP = 8
MB = 2
DOC = 256
STEP = 10
SEQS = 2
SEQ_LEN = 1536
TOKENS = 6144


def draw_segments(key, part):
    key = jax.random.fold_in(key, 7)
    pick_key, shift_key = jax.random.split(key)
    doc_count = SEQ_LEN // DOC
    whole_pick = jax.random.randint(pick_key, (SEQS,), 0, MB)
    shifts = jax.random.randint(shift_key, (MB, SEQS, doc_count // 2), -(3 * DOC // 4), 3 * DOC // 4 + 1)
    lengths = jnp.stack([DOC + shifts, DOC - shifts], axis=-1).reshape(MB, SEQS, doc_count)
    doc_ends = jnp.cumsum(lengths, axis=-1)
    positions = jnp.arange(SEQ_LEN, dtype=jnp.int32)
    numbers = jnp.sum((doc_ends[:, :, None, :] <= positions[None, None, :, None]).astype(jnp.int32), axis=-1)
    whole_mask = jnp.arange(MB, dtype=jnp.int32)[:, None, None] == whole_pick[None, :, None]
    return jnp.where(whole_mask, 0, numbers).astype(jnp.int32)


def block_scale(own_key, shape, cuts, least, largest):
    level, own = 1.0, jax.random.fold_in(own_key, 6)
    for axis_at, shards_of in cuts:
        draws = jnp.exp(jax.random.uniform(jax.random.fold_in(own, axis_at), (shards_of,), jnp.float32, least / len(cuts), largest / len(cuts)))
        level = level * jnp.repeat(draws, shape[axis_at] // shards_of).reshape([-1 if axis == axis_at else 1 for axis in range(len(shape))])
    return level


def distinct(rng, rows, number_of, top, lift):
    ranking = jax.random.permutation(jax.random.fold_in(rng, 1), number_of)
    favour = ranking
    for power in range(3):
        favour = favour * favour // number_of
    favour = favour * lift // number_of
    tickets = jax.random.randint(jax.random.fold_in(rng, 2), (rows, number_of), 0, 4096) + favour
    sure = jax.random.permutation(jax.random.fold_in(rng, 3), rows)[jnp.arange(number_of) % rows]
    tickets = jnp.where(jnp.arange(rows)[:, None] == sure[None, :], 1 << 14, tickets)
    priority = tickets * number_of + jnp.arange(number_of)
    return lax.top_k(priority.astype(jnp.int32), top)[1].astype(jnp.int32)


def gaussian(key, dims, scale, reach, cuts=(), kind=jnp.bfloat16):
    loudness = block_scale(key, dims, cuts, -0.22, 0.18) if cuts else 1.0
    entries = jax.random.normal(key, dims, jnp.float32) * scale * loudness
    return jnp.minimum(jnp.maximum(entries, -reach), reach).astype(kind)


def setup_inputs(seed: int = 0) -> dict:
    key_of = jax.random.split(jax.random.key(seed), 26)
    inputs = gaussian(key_of[0], (MB, SEQS, SEQ_LEN, D), 1.0, 6.0, ((1, 2), (2, 16)))
    cotangent = gaussian(key_of[1], (MB, SEQS, SEQ_LEN, D), 1.0, 6.0, ((1, 2), (2, 16)))
    routes = distinct(key_of[2], MB * SEQS * SEQ_LEN, EXPERTS, TOP, 4096).reshape((MB, SEQS, SEQ_LEN, TOP))
    segments = draw_segments(jax.random.fold_in(key_of[25], 71), 0)
    gains = jnp.clip(1.0 + 0.1 * jax.random.normal(key_of[4], (2, D), jnp.float32), 0.5, 1.5)
    gains_first = gaussian(key_of[5], (2, D), (0.16 * TOKENS ** 0.5), 80.0, ((1, 32),), jnp.float32)
    gains_second = jnp.clip(jnp.exp(math.log(5836.8) - 2.796019 * jax.random.uniform(key_of[6], (2, D), jnp.float32) ** block_scale(key_of[6], (2, D), ((1, 32),), -0.2, 0.2)), 356.352, 5836.8)
    w_query = gaussian(key_of[7], (D, HEADS * HEAD_DIM), D ** -0.5, 0.1875, ((0, 32),), jnp.float32)
    query_first = gaussian(key_of[8], (D, HEADS * HEAD_DIM), (0.16 * TOKENS ** 0.5), 80.0, ((0, 32),), jnp.float32)
    query_second = jnp.clip(jnp.exp(math.log(5836.8) - 2.796019 * jax.random.uniform(key_of[9], (D, HEADS * HEAD_DIM), jnp.float32) ** block_scale(key_of[9], (D, HEADS * HEAD_DIM), ((0, 32),), -0.2, 0.2)), 356.352, 5836.8)
    w_keyvalue = gaussian(key_of[10], (D, 2 * KV_HEADS * HEAD_DIM), D ** -0.5, 0.1875, ((0, 32),), jnp.float32)
    keyvalue_first = gaussian(key_of[11], (D, 2 * KV_HEADS * HEAD_DIM), (0.16 * TOKENS ** 0.5), 80.0, ((0, 32),), jnp.float32)
    keyvalue_second = jnp.clip(jnp.exp(math.log(5836.8) - 2.796019 * jax.random.uniform(key_of[12], (D, 2 * KV_HEADS * HEAD_DIM), jnp.float32) ** block_scale(key_of[12], (D, 2 * KV_HEADS * HEAD_DIM), ((0, 32),), -0.2, 0.2)), 356.352, 5836.8)
    w_out = gaussian(key_of[13], (D, HEADS * HEAD_DIM), (HEADS * HEAD_DIM // 64) ** -0.5, 1.5, ((0, 32),), jnp.float32)
    out_first = gaussian(key_of[14], (D, HEADS * HEAD_DIM), (0.011 * TOKENS ** 0.5), 5.0, ((0, 32),), jnp.float32)
    out_second = jnp.clip(jnp.exp(math.log(25.8048) - 2.7821582 * jax.random.uniform(key_of[15], (D, HEADS * HEAD_DIM), jnp.float32) ** block_scale(key_of[15], (D, HEADS * HEAD_DIM), ((0, 32),), -0.2, 0.2)), 1.59744, 25.8048)
    w_router = gaussian(key_of[16], (D, EXPERTS), (4 * D) ** -0.5, 0.09375, ((0, 32),), jnp.float32)
    router_first = gaussian(key_of[17], (D, EXPERTS), (0.77 * TOKENS ** 0.5), 384.0, ((0, 32),), jnp.float32)
    router_second = jnp.clip(jnp.exp(math.log(126566.4) - 2.7862742 * jax.random.uniform(key_of[18], (D, EXPERTS), jnp.float32) ** block_scale(key_of[18], (D, EXPERTS), ((0, 32),), -0.2, 0.2)), 7802.88, 126566.4)
    w_gate_up = gaussian(key_of[19], (EXPERTS, D, 2 * FF), D ** -0.5, 0.1875, ((1, 32),), jnp.float32)
    gate_up_first = gaussian(key_of[20], (EXPERTS, D, 2 * FF), (0.0385 * TOKENS ** 0.5), 16.0, ((1, 32),), jnp.float32)
    gate_up_second = jnp.clip(jnp.exp(math.log(313.344) - 2.7686748 * jax.random.uniform(key_of[21], (EXPERTS, D, 2 * FF), jnp.float32) ** block_scale(key_of[21], (EXPERTS, D, 2 * FF), ((1, 32),), -0.2, 0.2)), 19.6608, 313.344)
    w_down = gaussian(key_of[22], (EXPERTS, D, FF), (FF // 16) ** -0.5, 1.0, ((1, 32),), jnp.float32)
    down_first = gaussian(key_of[23], (EXPERTS, D, FF), (0.0066 * TOKENS ** 0.5), 3.0, ((1, 32),), jnp.float32)
    down_second = jnp.clip(jnp.exp(math.log(9.216) - 2.7699256 * jax.random.uniform(key_of[24], (EXPERTS, D, FF), jnp.float32) ** block_scale(key_of[24], (EXPERTS, D, FF), ((1, 32),), -0.2, 0.2)), 0.577536, 9.216)
    return {"inputs": inputs, "cotangent": cotangent, "routes": routes, "segments": segments, "gains": gains, "gains_first": gains_first, "gains_second": gains_second, "w_query": w_query, "query_first": query_first, "query_second": query_second, "w_keyvalue": w_keyvalue, "keyvalue_first": keyvalue_first, "keyvalue_second": keyvalue_second, "w_out": w_out, "out_first": out_first, "out_second": out_second, "w_router": w_router, "router_first": router_first, "router_second": router_second, "w_gate_up": w_gate_up, "gate_up_first": gate_up_first, "gate_up_second": gate_up_second, "w_down": w_down, "down_first": down_first, "down_second": down_second}


@jax.custom_vjp
def low(v):
    return lax.optimization_barrier(v.astype(jnp.bfloat16)).astype(jnp.float32)

@jax.custom_vjp
def low_back(v):
    return v

def low_keep(v):
    return (low(v), None)

def low_pass(kept, grad):
    return (grad,)

def back_keep(v):
    return (v, None)

def back_low(kept, grad):
    return (low(grad),)
low.defvjp(low_keep, low_pass)
low_back.defvjp(back_keep, back_low)
EPS_NORM = 1e-06
EPS_ADAM = 1e-08
BETA_ONE = 0.9
BETA_TWO = 0.95
MASKED = -1e+30
ROPE_BASE = 10000.0
RATES = (1.0, 0.04, 0.1, 1.5, 0.02, 0.1, 0.2)
DECAYS = (0.0, 0.1, 0.1, 0.1, 0.1, 0.1, 0.1)
HIGHEST = lax.Precision.HIGHEST

def rope_tables(positions):
    half_width = HEAD_DIM // 2
    frequency = ROPE_BASE ** (-(jnp.arange(half_width, dtype=jnp.float32) * 2.0) / HEAD_DIM)
    angles = positions.astype(jnp.float32)[:, None] * frequency[None, :]
    return (jnp.cos(angles), jnp.sin(angles))

def rotate(values, cosine_table, sine_table):
    half_width = values.shape[-1] // 2
    first_half = values[..., :half_width]
    second_half = values[..., half_width:]
    cos_rows = cosine_table[:, None, :]
    sin_rows = sine_table[:, None, :]
    return jnp.concatenate([first_half * cos_rows - second_half * sin_rows, second_half * cos_rows + first_half * sin_rows], axis=-1)

def normalize(values, gain):
    factor = lax.rsqrt(lax.optimization_barrier(jnp.mean(values * values, axis=-1, keepdims=True)) + EPS_NORM)
    return values * factor * gain

def attend_block(query_block, block_start, key_rows, value_rows, segment_row):
    row_count = query_block.shape[0]
    group_size = HEADS // KV_HEADS
    query_pos = block_start + jnp.arange(row_count, dtype=jnp.int32)
    key_pos = jnp.arange(key_rows.shape[0], dtype=jnp.int32)
    query_seg = lax.dynamic_slice_in_dim(segment_row, block_start, row_count)
    allowed = (query_seg[:, None] == segment_row[None, :]) & (query_pos[:, None] >= key_pos[None, :])
    grouped = query_block.reshape(row_count, KV_HEADS, group_size, HEAD_DIM)
    scores = jnp.einsum('cgrd,kgd->grck', grouped, key_rows, precision=HIGHEST) * HEAD_DIM ** (-0.5)
    scores = low_back(scores)
    scores = jnp.where(allowed[None, None], scores, MASKED)
    weights = low(jax.nn.softmax(scores, axis=-1))
    mixture = jnp.einsum('grck,kgd->cgrd', weights, value_rows, precision=HIGHEST)
    return mixture.reshape(row_count, HEADS * HEAD_DIM)

def layer_sequence(tokens, weights, routes_row, segment_row):
    gains, w_query, w_keyvalue, w_out, w_router, w_gate_up, w_down = weights
    length = tokens.shape[0]
    kv_width = KV_HEADS * HEAD_DIM
    cosine_table, sine_table = rope_tables(jnp.arange(length, dtype=jnp.int32))
    normed = low(normalize(tokens, gains[0]))
    query_raw = low_back(jnp.dot(normed, w_query, precision=HIGHEST))
    keyvalue_raw = low_back(jnp.dot(normed, w_keyvalue, precision=HIGHEST))
    queries = low(rotate(query_raw.reshape(length, HEADS, HEAD_DIM), cosine_table, sine_table))
    key_rows = low(rotate(keyvalue_raw[:, :kv_width].reshape(length, KV_HEADS, HEAD_DIM), cosine_table, sine_table))
    value_rows = low(keyvalue_raw[:, kv_width:].reshape(length, KV_HEADS, HEAD_DIM))
    block_rows = math.gcd(length, 512)
    starts = jnp.arange(length // block_rows, dtype=jnp.int32) * block_rows

    def one_block(pieces):
        return jax.checkpoint(attend_block)(pieces[0], pieces[1], key_rows, value_rows, segment_row)
    attended = lax.map(one_block, (queries.reshape(length // block_rows, block_rows, HEADS, HEAD_DIM), starts))
    attended = low(low_back(attended.reshape(length, HEADS * HEAD_DIM)))
    branch = low_back(jnp.dot(attended, w_out.T, precision=HIGHEST))
    middle = tokens + branch
    normed_ffn = low(normalize(middle, gains[1]))
    logits = jnp.dot(normed_ffn, w_router, precision=HIGHEST)
    selection = (routes_row[:, :, None] == jnp.arange(EXPERTS, dtype=jnp.int32)[None, None, :]).astype(jnp.float32)
    chosen = lax.optimization_barrier(jnp.sum(selection * logits[:, None, :], axis=-1))
    shares = jax.nn.softmax(chosen, axis=-1)
    gate_table = lax.optimization_barrier(jnp.sum(shares[:, :, None] * selection, axis=1))

    def expert_term(running, pieces):
        gate_up, down_proj, gate_column = pieces
        gate_and_up = low_back(jnp.dot(normed_ffn, gate_up, precision=HIGHEST))
        active = jax.nn.silu(gate_and_up[:, :FF]) * gate_and_up[:, FF:]
        scaled = low(gate_column[:, None] * active)
        return (running + jnp.dot(scaled, down_proj.T, precision=HIGHEST), None)
    expert_sum, _ = lax.scan(jax.checkpoint(expert_term), jnp.zeros_like(tokens), (w_gate_up, w_down, gate_table.T))
    return middle + low_back(expert_sum)

def forward_all(tokens_all, weight_list, routes_all, segments_all):
    lowered = tuple((low(weight) for weight in weight_list))

    def one_sequence(pieces):
        return jax.checkpoint(layer_sequence)(pieces[0], lowered, pieces[1], pieces[2])
    return lax.map(one_sequence, (tokens_all, routes_all, segments_all))

def adamw_step(weight, gradient, moment, second, step_rate, decay_rate):
    moment_new = BETA_ONE * moment + (1.0 - BETA_ONE) * gradient
    second_new = BETA_TWO * second + (1.0 - BETA_TWO) * gradient * gradient
    moment_hat = moment_new / (1.0 - BETA_ONE ** STEP)
    second_hat = second_new / (1.0 - BETA_TWO ** STEP)
    weight_new = weight - step_rate * (moment_hat / (jnp.sqrt(second_hat) + EPS_ADAM) + decay_rate * weight)
    return (moment_new, second_new, weight_new)

def reference(inputs, cotangent, routes, segments, gains, gains_first, gains_second, w_query, query_first, query_second, w_keyvalue, keyvalue_first, keyvalue_second, w_out, out_first, out_second, w_router, router_first, router_second, w_gate_up, gate_up_first, gate_up_second, w_down, down_first, down_second):
    full_shape = inputs.shape
    seq_count = full_shape[0] * full_shape[1]
    flat_inputs = inputs.astype(jnp.float32).reshape(seq_count, full_shape[2], full_shape[3])
    flat_routes = routes.reshape(seq_count, full_shape[2], TOP)
    flat_segments = segments.reshape(seq_count, full_shape[2])
    weights = (gains, w_query, w_keyvalue, w_out, w_router, w_gate_up, w_down)
    firsts = (gains_first, query_first, keyvalue_first, out_first, router_first, gate_up_first, down_first)
    seconds = (gains_second, query_second, keyvalue_second, out_second, router_second, gate_up_second, down_second)

    def forward_flat(tokens_all, *weight_list):
        return forward_all(tokens_all, weight_list, flat_routes, flat_segments)
    result, pullback = jax.vjp(forward_flat, flat_inputs, *weights)
    gradients = pullback(cotangent.astype(jnp.float32).reshape(result.shape))
    outputs = result.astype(jnp.bfloat16).reshape(full_shape)
    input_grad = gradients[0].reshape(full_shape)
    updated = []
    for kind_index in range(7):
        updated.extend(adamw_step(weights[kind_index], gradients[kind_index + 1], firsts[kind_index], seconds[kind_index], RATES[kind_index], DECAYS[kind_index]))
    gains_moment, gains_square, gains_new, query_moment, query_square, query_new, keyvalue_moment, keyvalue_square, keyvalue_new, out_moment, out_square, out_new, router_moment, router_square, router_new, gate_up_moment, gate_up_square, gate_up_new, down_moment, down_square, down_new = updated
    return (outputs, input_grad, gains_moment, gains_square, gains_new, query_moment, query_square, query_new, keyvalue_moment, keyvalue_square, keyvalue_new, out_moment, out_square, out_new, router_moment, router_square, router_new, gate_up_moment, gate_up_square, gate_up_new, down_moment, down_square, down_new)
```

```python
import math

import jax
import jax.numpy as jnp
from jax import lax
from jax.sharding import PartitionSpec as P

HEADS = 16
KV_HEADS = 8
HEAD_DIM = 64
FF = 512
EXPERTS = 16
STEP = 10


EPS_NORM = 1e-06
EPS_ADAM = 1e-08
BETA_ONE = 0.9
BETA_TWO = 0.95
MASKED = -1e30
ROPE_BASE = 10000.0
RATES = (1.0, 0.04, 0.1, 1.5, 0.02, 0.1, 0.2)
DECAYS = (0.0, 0.1, 0.1, 0.1, 0.1, 0.1, 0.1)
HIGHEST = lax.Precision.HIGHEST


def rope_tables(positions):
    half_width = HEAD_DIM // 2
    frequency = ROPE_BASE ** (-(jnp.arange(half_width, dtype=jnp.float32) * 2.0) / HEAD_DIM)
    angles = positions.astype(jnp.float32)[:, None] * frequency[None, :]
    return (jnp.cos(angles), jnp.sin(angles))


def rotate(values, cosine_table, sine_table):
    half_width = values.shape[-1] // 2
    first_half = values[..., :half_width]
    second_half = values[..., half_width:]
    cos_rows = cosine_table[:, None, :]
    sin_rows = sine_table[:, None, :]
    return jnp.concatenate(
        [
            first_half * cos_rows - second_half * sin_rows,
            second_half * cos_rows + first_half * sin_rows,
        ],
        axis=-1,
    )


def prepare_blocks(shard_rows):
    total_rows = shard_rows.shape[0]
    step_rows = math.gcd(total_rows, 512)
    blocks = shard_rows.reshape(total_rows // step_rows, step_rows, shard_rows.shape[1])
    offsets = jnp.arange(total_rows // step_rows, dtype=jnp.int32) * step_rows
    return (blocks, offsets, step_rows)


def block_scores(grouped, block_rows, key_start, step_rows, query_seg, query_pos, segment_row):
    kv_width = KV_HEADS * HEAD_DIM
    key_rows = block_rows[:, :kv_width].reshape(step_rows, KV_HEADS, HEAD_DIM)
    value_rows = block_rows[:, kv_width:].reshape(step_rows, KV_HEADS, HEAD_DIM)
    key_seg = lax.dynamic_slice_in_dim(segment_row, key_start, step_rows)
    key_pos = key_start + jnp.arange(step_rows, dtype=jnp.int32)
    allowed = ((query_seg[:, None] == key_seg[None, :]) & (query_pos[:, None] >= key_pos[None, :]))[
        None, None
    ]
    scores = jnp.einsum(
        "cgrd,kgd->grck", grouped, key_rows, preferred_element_type=jnp.float32
    ) * HEAD_DIM ** (-0.5)
    return (key_rows, value_rows, allowed, jnp.where(allowed, scores, MASKED))


def fold_forward(running, shard_rows, grouped, query_seg, query_pos, segment_row, limit):
    blocks, offsets, step_rows = prepare_blocks(shard_rows)

    def visit(current, block_pair):
        block_rows, offset = block_pair

        def attend(inner):
            maxima, totals, accumulated = inner
            key_rows, value_rows, allowed, scores = block_scores(
                grouped, block_rows, offset, step_rows, query_seg, query_pos, segment_row
            )
            new_max = jnp.maximum(maxima, jnp.max(scores, axis=-1))
            fading = jnp.exp(maxima - new_max)
            block_weights = jnp.where(allowed, jnp.exp(scores - new_max[..., None]), 0.0)
            totals = totals * fading + jnp.sum(block_weights, axis=-1)
            update = jnp.einsum(
                "grck,kgd->cgrd",
                block_weights.astype(jnp.bfloat16),
                value_rows,
                preferred_element_type=jnp.float32,
            )
            accumulated = accumulated * jnp.transpose(fading, (2, 0, 1))[..., None] + update
            return (new_max, totals, accumulated)

        return (lax.cond(offset < limit, attend, lambda inner: inner, current), None)

    running, unused = lax.scan(visit, running, (blocks, offsets))
    return running


def fold_backward(
    running,
    shard_rows,
    grouped,
    grad_grouped,
    log_totals,
    deltas,
    query_seg,
    query_pos,
    segment_row,
    limit,
):
    blocks, offsets, step_rows = prepare_blocks(shard_rows)
    kv_width = KV_HEADS * HEAD_DIM
    factor = HEAD_DIM ** (-0.5)

    def visit(current, block_pair):
        block_rows, offset = block_pair

        def attend(inner):
            grad_query, grad_keys = inner
            key_rows, value_rows, allowed, scores = block_scores(
                grouped, block_rows, offset, step_rows, query_seg, query_pos, segment_row
            )
            block_weights = jnp.where(allowed, jnp.exp(scores - log_totals[..., None]), 0.0)
            grad_weights = jnp.einsum(
                "cgrd,kgd->grck", grad_grouped, value_rows, preferred_element_type=jnp.float32
            )
            grad_scores = (block_weights * (grad_weights - deltas[..., None])).astype(jnp.bfloat16)
            grad_query = (
                grad_query
                + jnp.einsum(
                    "grck,kgd->cgrd", grad_scores, key_rows, preferred_element_type=jnp.float32
                )
                * factor
            )
            key_part = (
                jnp.einsum(
                    "grck,cgrd->kgd", grad_scores, grouped, preferred_element_type=jnp.float32
                )
                * factor
            )
            value_part = jnp.einsum(
                "grck,cgrd->kgd",
                block_weights.astype(jnp.bfloat16),
                grad_grouped,
                preferred_element_type=jnp.float32,
            )
            block_grad = jnp.concatenate(
                [key_part.reshape(step_rows, kv_width), value_part.reshape(step_rows, kv_width)],
                axis=1,
            )
            previous = lax.dynamic_slice_in_dim(grad_keys, offset, step_rows, 0)
            grad_keys = lax.dynamic_update_slice_in_dim(grad_keys, previous + block_grad, offset, 0)
            return (grad_query, grad_keys)

        return (lax.cond(offset < limit, attend, lambda inner: inner, current), None)

    running, unused = lax.scan(visit, running, (blocks, offsets))
    return running


def halving_start(partial, axis_name, axis):
    count = lax.axis_size(axis_name)
    bits = count.bit_length() - 1
    shape = partial.shape
    block = shape[axis] // count
    value = partial.reshape(shape[:axis] + (2,) * bits + (block,) + shape[axis + 1 :])
    return (value, axis, tuple(range(bits - 1, -1, -1)))


def halving_step(state, axis_name, bit):
    value, axis, left = state
    count = lax.axis_size(axis_name)
    place = axis + left.index(bit)
    left = tuple(other for other in left if other != bit)
    mine = (lax.axis_index(axis_name) >> bit) & 1
    pairs = [(i, i ^ (1 << bit)) for i in range(count)]
    away = lax.dynamic_index_in_dim(value, 1 - mine, place, keepdims=False)
    arrived = lax.ppermute(away, axis_name, pairs)
    kept = lax.dynamic_index_in_dim(value, mine, place, keepdims=False)
    value = kept.astype(jnp.float32) + arrived.astype(jnp.float32)
    if left:
        value = value.astype(jnp.bfloat16)
    return (value, axis, left)


def halving_sum(partial, axis_name, axis, bit_order):
    count = lax.axis_size(axis_name)
    if count & (count - 1):
        owned = lax.psum_scatter(partial, axis_name, scatter_dimension=axis, tiled=True)
        return owned.astype(jnp.float32)
    state = halving_start(partial, axis_name, axis)
    for bit in bit_order:
        state = halving_step(state, axis_name, bit)
    return state[0].astype(jnp.float32)


def orders_of(count):
    bits = tuple(range(count.bit_length() - 1))
    first, second, rest = bits[:1], bits[1:2], bits[2:]
    return (bits, second + rest + first, rest[:1] + first + second + rest[1:])


def core_gradient(features, columns):
    width = features.shape[1]
    if lax.axis_size("batch") != 2:
        whole = lax.dot_general(
            features, columns, (((0,), (0,)), ((), ())), preferred_element_type=jnp.float32
        ).astype(jnp.bfloat16)
        return halving_sum(
            whole, "batch", 0, tuple(range(lax.axis_size("batch").bit_length() - 1))
        ).astype(jnp.bfloat16)
    core = lax.axis_index("batch")

    def rows_of(which):
        part = lax.dynamic_slice_in_dim(features, which * (width // 2), width // 2, 1)
        return lax.dot_general(
            part, columns, (((0,), (0,)), ((), ())), preferred_element_type=jnp.float32
        ).astype(jnp.bfloat16)

    arrived = lax.ppermute(rows_of(1 - core), "batch", [(0, 1), (1, 0)])
    kept = rows_of(core)
    return (kept.astype(jnp.float32) + arrived.astype(jnp.float32)).astype(jnp.bfloat16)


def weight_gradient(features, columns, order):
    return halving_sum(core_gradient(features, columns), "ctx", 0, order)


def route_gates(normed_rows, router_low, route_rows):
    logits = jnp.dot(normed_rows, router_low, preferred_element_type=jnp.float32)
    selection = (
        route_rows[:, :, None] == jnp.arange(EXPERTS, dtype=jnp.int32)[None, None, :]
    ).astype(jnp.float32)
    chosen = jnp.sum(selection * logits[:, None, :], axis=-1)
    shares = jax.nn.softmax(chosen, axis=-1)
    gate_table = jnp.sum(shares[:, :, None] * selection, axis=1)
    return (selection, shares, gate_table)


def swiglu_back(grad_active, gate_part, up_part):
    sigmoid_gate = jax.nn.sigmoid(gate_part)
    grad_gate = grad_active * up_part * sigmoid_gate * (1.0 + gate_part * (1.0 - sigmoid_gate))
    grad_up = grad_active * gate_part * sigmoid_gate
    return (grad_gate, grad_up)


def dot_t(left, right):
    return lax.dot_general(
        left, right, (((1,), (1,)), ((), ())), preferred_element_type=jnp.float32
    )


def adamw_step(weight, gradient, moment, second, step_rate, decay_rate):
    moment_new = BETA_ONE * moment + (1.0 - BETA_ONE) * gradient
    second_new = BETA_TWO * second + (1.0 - BETA_TWO) * gradient * gradient
    moment_hat = moment_new / (1.0 - BETA_ONE**STEP)
    second_hat = second_new / (1.0 - BETA_TWO**STEP)
    weight_new = weight - step_rate * (
        moment_hat / (jnp.sqrt(second_hat) + EPS_ADAM) + decay_rate * weight
    )
    return (moment_new, second_new, weight_new)


def body(
    inputs,
    cotangent,
    routes,
    segments,
    gains,
    gains_first,
    gains_second,
    w_query,
    query_first,
    query_second,
    w_keyvalue,
    keyvalue_first,
    keyvalue_second,
    w_out,
    out_first,
    out_second,
    w_router,
    router_first,
    router_second,
    w_gate_up,
    gate_up_first,
    gate_up_second,
    w_down,
    down_first,
    down_second,
):
    micro_count, unused, span_rows, width = inputs.shape
    rows = micro_count * span_rows
    kv_width = KV_HEADS * HEAD_DIM
    q_width = HEADS * HEAD_DIM
    group_size = HEADS // KV_HEADS
    ctx_count = lax.axis_size("ctx")
    order_a, order_b, order_c = orders_of(ctx_count)
    anchor = lax.axis_index("ctx") * span_rows
    cosine_table, sine_table = rope_tables(anchor + jnp.arange(span_rows, dtype=jnp.int32))
    cosine_table = jnp.tile(cosine_table, (micro_count, 1))
    sine_table = jnp.tile(sine_table, (micro_count, 1))
    weights = (gains, w_query, w_keyvalue, w_out, w_router, w_gate_up, w_down)
    firsts = (
        gains_first,
        query_first,
        keyvalue_first,
        out_first,
        router_first,
        gate_up_first,
        down_first,
    )
    seconds = (
        gains_second,
        query_second,
        keyvalue_second,
        out_second,
        router_second,
        gate_up_second,
        down_second,
    )
    everyone = ("batch", "ctx")
    own_rows = w_query.shape[0]
    dense_pack = jnp.concatenate(
        [
            w_query,
            w_keyvalue,
            w_out,
            w_router,
            gains.T,
            jnp.zeros((own_rows, 128 - EXPERTS - 2), jnp.float32),
        ],
        axis=1,
    ).astype(jnp.bfloat16)
    dense_all = lax.all_gather(dense_pack, everyone, axis=0, tiled=True)
    gate_up_flat = jnp.transpose(w_gate_up.astype(jnp.bfloat16), (1, 0, 2)).reshape(own_rows, -1)
    down_flat = jnp.transpose(w_down.astype(jnp.bfloat16), (1, 0, 2)).reshape(own_rows, -1)

    down_flat, dense_all = lax.optimization_barrier((down_flat, dense_all))
    down_low = lax.all_gather(down_flat, everyone, axis=0, tiled=True)
    qkv_low = dense_all[:, : q_width + 2 * kv_width]
    out_low = dense_all[:, q_width + 2 * kv_width : 2 * q_width + 2 * kv_width]
    tail = dense_all[:, 2 * q_width + 2 * kv_width :]
    router_low = tail[:, :EXPERTS]
    gain_attn = tail[:, EXPERTS].astype(jnp.float32)
    gain_ffn = tail[:, EXPERTS + 1].astype(jnp.float32)

    tokens = inputs.reshape(rows, width).astype(jnp.float32)
    cot_rows = cotangent.reshape(rows, width)
    route_rows = lax.dynamic_slice_in_dim(routes[:, 0], anchor, span_rows, 1).reshape(rows, -1)

    inv_first = lax.rsqrt(jnp.mean(tokens * tokens, axis=-1, keepdims=True) + EPS_NORM)
    unit_first = tokens * inv_first
    normed = (unit_first * gain_attn).astype(jnp.bfloat16)
    raw = jnp.dot(normed, qkv_low, preferred_element_type=jnp.float32)
    queries = rotate(
        raw[:, :q_width].reshape(rows, HEADS, HEAD_DIM), cosine_table, sine_table
    ).astype(jnp.bfloat16)
    key_rows = rotate(
        raw[:, q_width : q_width + kv_width].reshape(rows, KV_HEADS, HEAD_DIM),
        cosine_table,
        sine_table,
    ).astype(jnp.bfloat16)
    shipped = jnp.concatenate(
        [key_rows.reshape(rows, kv_width), raw[:, q_width + kv_width :].astype(jnp.bfloat16)],
        axis=1,
    ).reshape(micro_count, span_rows, 2 * kv_width)
    shipped, down_low = lax.optimization_barrier((shipped, down_low))
    shipped_all = lax.all_gather(shipped, "ctx", axis=1, tiled=True)
    gate_up_flat, shipped_all = lax.optimization_barrier((gate_up_flat, shipped_all))
    gate_up_low = lax.all_gather(gate_up_flat, everyone, axis=0, tiled=True)

    grouped = queries.reshape(micro_count, span_rows, KV_HEADS, group_size, HEAD_DIM)
    query_pos = anchor + jnp.arange(span_rows, dtype=jnp.int32)
    limit = anchor + span_rows
    attended_list = []
    log_list = []
    for micro_index in range(micro_count):
        segment_row = segments[micro_index, 0]
        maxima, totals, accumulated = fold_forward(
            (
                jnp.full((KV_HEADS, group_size, span_rows), MASKED, jnp.float32),
                jnp.zeros((KV_HEADS, group_size, span_rows), jnp.float32),
                jnp.zeros((span_rows, KV_HEADS, group_size, HEAD_DIM), jnp.float32),
            ),
            shipped_all[micro_index],
            grouped[micro_index],
            lax.dynamic_slice_in_dim(segment_row, anchor, span_rows),
            query_pos,
            segment_row,
            limit,
        )
        attended_list.append(
            (accumulated / jnp.transpose(totals, (2, 0, 1))[..., None]).reshape(span_rows, q_width)
        )
        log_list.append(maxima + jnp.log(totals))
    attended = jnp.concatenate(attended_list, axis=0)
    attended_low = attended.astype(jnp.bfloat16)
    middle = tokens + dot_t(attended_low, out_low)
    inv_second = lax.rsqrt(jnp.mean(middle * middle, axis=-1, keepdims=True) + EPS_NORM)
    unit_second = middle * inv_second
    normed_ffn = (unit_second * gain_ffn).astype(jnp.bfloat16)

    selection, shares, gate_table = route_gates(normed_ffn, router_low, route_rows)
    gate_and_up = jnp.dot(normed_ffn, gate_up_low, preferred_element_type=jnp.float32).reshape(
        rows, EXPERTS, 2 * FF
    )
    gate_part, up_part = gate_and_up[..., :FF], gate_and_up[..., FF:]
    active = jax.nn.silu(gate_part) * up_part
    scaled = (gate_table[:, :, None] * active).astype(jnp.bfloat16).reshape(rows, EXPERTS * FF)
    outputs = (middle + dot_t(scaled, down_low)).astype(jnp.bfloat16).reshape(inputs.shape)
    down_half = core_gradient(cot_rows, scaled)

    grad_scaled = jnp.dot(cot_rows, down_low, preferred_element_type=jnp.float32).reshape(
        rows, EXPERTS, FF
    )
    grad_gate_table = jnp.sum(grad_scaled * active, axis=-1)
    grad_gate, grad_up = swiglu_back(gate_table[:, :, None] * grad_scaled, gate_part, up_part)
    grad_both = (
        jnp.concatenate([grad_gate, grad_up], axis=-1)
        .astype(jnp.bfloat16)
        .reshape(rows, EXPERTS * 2 * FF)
    )
    middle_column = EXPERTS * FF
    halves = (
        core_gradient(normed_ffn, grad_both[:, :middle_column]),
        core_gradient(normed_ffn, grad_both[:, middle_column:]),
        down_half,
    )
    grad_normed_part = dot_t(grad_both, gate_up_low)
    orders = (order_a, order_b, order_c)
    stepwise = ctx_count & (ctx_count - 1) == 0
    grad_normed_part, halves = lax.optimization_barrier((grad_normed_part, halves))
    if stepwise:
        states = [halving_start(half, "ctx", 0) for half in halves]
    done_steps = 0

    grad_shares = jnp.sum(grad_gate_table[:, None, :] * selection, axis=-1)
    grad_chosen = shares * (grad_shares - jnp.sum(shares * grad_shares, axis=-1, keepdims=True))
    grad_logits = jnp.sum(grad_chosen[:, :, None] * selection, axis=1)
    grad_normed_ffn = grad_normed_part + jnp.dot(
        grad_logits, router_low.astype(jnp.float32).T, precision=HIGHEST
    )
    grad_router = jnp.dot(normed_ffn.astype(jnp.float32).T, grad_logits, precision=HIGHEST)
    scaled_ffn = grad_normed_ffn * gain_ffn
    grad_gain_ffn = jnp.sum(grad_normed_ffn * unit_second, axis=0)
    grad_middle = cot_rows.astype(jnp.float32) + inv_second * (
        scaled_ffn - unit_second * jnp.mean(scaled_ffn * unit_second, axis=-1, keepdims=True)
    )
    grad_branch = grad_middle.astype(jnp.bfloat16)
    grad_attended = jnp.dot(grad_branch, out_low, preferred_element_type=jnp.float32).astype(
        jnp.bfloat16
    )
    grad_grouped = grad_attended.reshape(micro_count, span_rows, KV_HEADS, group_size, HEAD_DIM)
    deltas = jnp.sum(
        (grad_attended.astype(jnp.float32) * attended).reshape(
            micro_count, span_rows, KV_HEADS, group_size, HEAD_DIM
        ),
        axis=-1,
    )
    grad_query_list = []
    grad_keys_list = []
    for micro_index in range(micro_count):
        segment_row = segments[micro_index, 0]
        grad_query_rot, grad_keys_all = fold_backward(
            (
                jnp.zeros((span_rows, KV_HEADS, group_size, HEAD_DIM), jnp.float32),
                jnp.zeros((segment_row.shape[0], 2 * kv_width), jnp.float32),
            ),
            shipped_all[micro_index],
            grouped[micro_index],
            grad_grouped[micro_index],
            log_list[micro_index],
            jnp.transpose(deltas[micro_index], (1, 2, 0)),
            lax.dynamic_slice_in_dim(segment_row, anchor, span_rows),
            query_pos,
            segment_row,
            limit,
        )
        if stepwise and done_steps < len(order_a) - 1:
            states = [
                halving_step(state, "ctx", order[done_steps])
                for state, order in zip(states, orders)
            ]
            done_steps += 1
            held, grad_query_rot, grad_keys_all, grad_grouped = lax.optimization_barrier(
                (tuple(state[0] for state in states), grad_query_rot, grad_keys_all, grad_grouped)
            )
            states = [(value,) + state[1:] for value, state in zip(held, states)]
        grad_query_list.append(grad_query_rot.reshape(span_rows, HEADS, HEAD_DIM))
        grad_keys_list.append(
            halving_sum(grad_keys_all.astype(jnp.bfloat16), "ctx", 0, (order_a, order_b)[micro_index % 2])
        )
    grad_shipped = jnp.concatenate(grad_keys_list, axis=0)
    grad_query_raw = rotate(
        jnp.concatenate(grad_query_list, axis=0), cosine_table, -sine_table
    ).reshape(rows, q_width)
    grad_key_raw = rotate(
        grad_shipped[:, :kv_width].reshape(rows, KV_HEADS, HEAD_DIM), cosine_table, -sine_table
    ).reshape(rows, kv_width)
    grad_raw = jnp.concatenate(
        [grad_query_raw, grad_key_raw, grad_shipped[:, kv_width:]], axis=1
    ).astype(jnp.bfloat16)
    grad_normed = dot_t(grad_raw, qkv_low)
    scaled_attn = grad_normed * gain_attn
    grad_gain_attn = jnp.sum(grad_normed * unit_first, axis=0)
    input_grads = (
        grad_middle
        + inv_first
        * (scaled_attn - unit_first * jnp.mean(scaled_attn * unit_first, axis=-1, keepdims=True))
    ).reshape(inputs.shape)
    out_owned = weight_gradient(grad_branch, attended_low, order_c)
    small = jnp.concatenate(
        [
            grad_router,
            grad_gain_attn[:, None],
            grad_gain_ffn[:, None],
            jnp.zeros((width, 128 - EXPERTS - 2), jnp.float32),
        ],
        axis=1,
    )
    if stepwise:
        owned_experts = []
        for state, order in zip(states, orders):
            for bit in order[done_steps:]:
                state = halving_step(state, "ctx", bit)
            owned_experts.append(state[0].astype(jnp.float32))
    else:
        owned_experts = [halving_sum(half, "ctx", 0, order_a) for half in halves]
    gate_up_owned = jnp.concatenate(owned_experts[:2], axis=1)
    down_owned = owned_experts[2]
    small_owned = lax.psum_scatter(small, everyone, scatter_dimension=0, tiled=True)
    raw_owned = weight_gradient(normed, grad_raw, order_a)
    owned_grads = (
        small_owned[:, EXPERTS : EXPERTS + 2].T,
        raw_owned[:, :q_width],
        raw_owned[:, q_width:],
        out_owned,
        small_owned[:, :EXPERTS],
        jnp.transpose(gate_up_owned.reshape(own_rows, EXPERTS, 2 * FF), (1, 0, 2)),
        jnp.transpose(down_owned.reshape(own_rows, EXPERTS, FF), (1, 0, 2)),
    )
    updated = []
    for kind_index in range(7):
        updated.extend(
            adamw_step(
                weights[kind_index],
                owned_grads[kind_index],
                firsts[kind_index],
                seconds[kind_index],
                RATES[kind_index],
                DECAYS[kind_index],
            )
        )
    (
        gains_moment,
        gains_square,
        gains_new,
        query_moment,
        query_square,
        query_new,
        keyvalue_moment,
        keyvalue_square,
        keyvalue_new,
        out_moment,
        out_square,
        out_new,
        router_moment,
        router_square,
        router_new,
        gate_up_moment,
        gate_up_square,
        gate_up_new,
        down_moment,
        down_square,
        down_new,
    ) = updated
    return (
        outputs,
        input_grads,
        gains_moment,
        gains_square,
        gains_new,
        query_moment,
        query_square,
        query_new,
        keyvalue_moment,
        keyvalue_square,
        keyvalue_new,
        out_moment,
        out_square,
        out_new,
        router_moment,
        router_square,
        router_new,
        gate_up_moment,
        gate_up_square,
        gate_up_new,
        down_moment,
        down_square,
        down_new,
    )


def solution(mesh):
    placed = (
        P(None, "batch", "ctx", None),
        P(None, "batch", "ctx", None),
        P(None, "batch", None, None),
        P(None, "batch", None),
        P(None, ("batch", "ctx")),
        P(None, ("batch", "ctx")),
        P(None, ("batch", "ctx")),
        P(("batch", "ctx"), None),
        P(("batch", "ctx"), None),
        P(("batch", "ctx"), None),
        P(("batch", "ctx"), None),
        P(("batch", "ctx"), None),
        P(("batch", "ctx"), None),
        P(("batch", "ctx"), None),
        P(("batch", "ctx"), None),
        P(("batch", "ctx"), None),
        P(("batch", "ctx"), None),
        P(("batch", "ctx"), None),
        P(("batch", "ctx"), None),
        P(None, ("batch", "ctx"), None),
        P(None, ("batch", "ctx"), None),
        P(None, ("batch", "ctx"), None),
        P(None, ("batch", "ctx"), None),
        P(None, ("batch", "ctx"), None),
        P(None, ("batch", "ctx"), None),
    )
    return jax.shard_map(
        body,
        mesh=mesh,
        in_specs=placed,
        out_specs=(
            P(None, "batch", "ctx", None),
            P(None, "batch", "ctx", None),
            P(None, ("batch", "ctx")),
            P(None, ("batch", "ctx")),
            P(None, ("batch", "ctx")),
            P(("batch", "ctx"), None),
            P(("batch", "ctx"), None),
            P(("batch", "ctx"), None),
            P(("batch", "ctx"), None),
            P(("batch", "ctx"), None),
            P(("batch", "ctx"), None),
            P(("batch", "ctx"), None),
            P(("batch", "ctx"), None),
            P(("batch", "ctx"), None),
            P(("batch", "ctx"), None),
            P(("batch", "ctx"), None),
            P(("batch", "ctx"), None),
            P(None, ("batch", "ctx"), None),
            P(None, ("batch", "ctx"), None),
            P(None, ("batch", "ctx"), None),
            P(None, ("batch", "ctx"), None),
            P(None, ("batch", "ctx"), None),
            P(None, ("batch", "ctx"), None),
        ),
        check_vma=False,
    )
```
